32 devices in a mesh: groups: 2 (over y), expert: 16 (over z, x, core).
Axes of the slice: x: 2, y: 2, z: 4, core: 2. Of those that a mesh axis runs over, the one named last changes fastest.
Arguments:
- routes: int32 [4096, 8], P(('groups', 'expert')), parts along dimension 0, may hold values from 0 to 15, all different within a row; in each aligned block of 128 rows (0 to 127, 128 to 255, ...) at most 128 rows name the same one
- acts: bfloat16 [4096, 2048], P(('groups', 'expert')), parts along dimension 0, may hold values from -36 to 36
- grads: bfloat16 [4096, 8, 768], P(('groups', 'expert')), parts along dimension 0, may hold values from -36 to 36
- weights: bfloat16 [32, 2048, 768], P(('groups', 'expert')), parts along dimension 0, may hold values from -6 to 6
- cluster: int32 [32], P('groups'), parts along dimension 0, may hold values from 0 to 7, as said below
Outputs:
- merged: float32 [16, 2048, 768], P('groups', 'expert'), parts along dimension 0
The draws below stay inside these ranges and needn't reach their ends.
There are 2 independent parts, one for each index of `groups`. The reference program is written for one: setup_inputs(seed, part) draws one part's arguments, and reference() takes and returns one part's arrays. A program takes and returns all parts, laid end to end along the dimension named above; each array names one. Nothing has to cross between parts.
Inputs may be any that keep to these rules, and one draw needn't show every extreme that they name: `routes`: in the rows of one device no expert is named by more than 128 pairs; every expert is named by some pair; a token names 8 different experts. `cluster`: every merged expert has exactly two members.
All inputs are finite; a program needn't handle non-finite values.
Results may differ from the reference program's by a relative error of at most 0.00056.
Values may be sent and summed in bfloat16 or wider, within the bound.
A program may use at most 128 MiB of HBM per device.

```python
import math
import jax
import jax.numpy as jnp
import numpy as np
from jax import lax

D = 2048
F = 768
TOP = 8
TOK_DEV = 128
EXPERTS = 16
CLUSTERS = 8
CAP = 128
TOKENS = 2048
N_EXPERT = 16


def rough_field(key, shape, row_shape, col_shape, spread):
    key_rows, key_cols, key_cells, key_base = jax.random.split(key, 4)
    row_scale = jnp.exp(jax.random.uniform(key_rows, row_shape, jnp.float32, math.log(0.5), math.log(1.6)))
    col_scale = jnp.exp(jax.random.uniform(key_cols, col_shape, jnp.float32, math.log(0.3), math.log(3.0)))
    cell_scale = jnp.exp(jax.random.uniform(key_cells, shape, jnp.float32, math.log(0.05), math.log(3.0)))
    base_draw = spread(key_base, shape)
    return jnp.clip(base_draw * row_scale * col_scale * cell_scale, -36.0, 36.0)


def normal_base(key, shape):
    return jax.random.truncated_normal(key, -4.0, 4.0, shape, jnp.float32)


def draw_acts(key, part):
    key = jax.random.fold_in(key, 11)
    values = rough_field(key, (TOKENS, D), (TOKENS, 1), (1, D), normal_base)
    return values.astype(jnp.bfloat16)


def draw_grads(key, part):
    key = jax.random.fold_in(key, 12)
    values = rough_field(key, (TOKENS, TOP, F), (TOKENS, TOP, 1), (1, 1, F), normal_base)
    return values.astype(jnp.bfloat16)


def draw_cluster(key, part):
    key = jax.random.fold_in(key, 13)
    shuffled = jax.random.permutation(key, EXPERTS).astype(jnp.int32)
    labels = jnp.arange(EXPERTS, dtype=jnp.int32) // 2
    return jnp.zeros((EXPERTS,), jnp.int32).at[shuffled].set(labels)


def levels(stream_key, extent, cuts, least, high):
    factor_of, own = 1.0, jax.random.fold_in(stream_key, 6)
    for dim, shards_of in cuts:
        heights = jnp.exp(jax.random.uniform(jax.random.fold_in(own, dim), (shards_of,), jnp.float32, least / len(cuts), high / len(cuts)))
        factor_of = factor_of * jnp.repeat(heights, extent[dim] // shards_of).reshape([-1 if axis == dim else 1 for axis in range(len(extent))])
    return factor_of


def deal_out(stream_key, own, number, rows, number_of, top, reach, skew):
    sequence = jax.random.permutation(stream_key, number_of)
    packed, usual = load_shares(number_of, rows * top, reach, skew, True), load_shares(number_of, rows * top, reach, skew, False)
    places = jnp.arange(number_of)

    def named(lengths, rotation):
        used = int((lengths > 0).sum())
        fixed = max(1, used // 4)
        moved = fixed + (places - fixed + rotation * (used - fixed)) % max(1, number_of - fixed)
        return jnp.zeros((number_of,), jnp.int32).at[sequence[jnp.where(places < fixed, places, moved)]].set(jnp.asarray(lengths, jnp.int32))

    lengths = jnp.where(number % 4 == 0, named(packed, number // 4), named(usual, number - number // 4 - 1))
    mixed = jax.random.permutation(jax.random.fold_in(own, 3), number_of)
    source_of, taker = mixed[0:number_of // 2 * 2:2], mixed[1:number_of // 2 * 2:2]
    room = jnp.minimum(lengths[source_of] - 1, reach - lengths[taker]) // 2
    room = jnp.where((source_of == sequence[0]) | (taker == sequence[0]) | (lengths[taker] == 0), 0, jnp.maximum(room, 0))
    moved = jax.random.randint(jax.random.fold_in(own, 4), (number_of // 2,), 0, 1 << 20) % (room + 1)
    lengths = lengths.at[source_of].add(-moved).at[taker].add(moved)
    items = jnp.searchsorted(jnp.cumsum(lengths), jnp.arange(rows * top), side="right").astype(jnp.int32)
    listing = items.reshape(top, rows).T
    listing = listing[jax.random.permutation(jax.random.fold_in(own, 1), rows)]
    rotation = jax.random.randint(jax.random.fold_in(own, 2), (rows, 1), 0, top)
    return jnp.take_along_axis(listing, (jnp.arange(top)[None, :] + rotation) % top, axis=1)


def load_shares(amount, total, reach, slope, full):
    portions = [(1 << 20) // math.isqrt(rank ** slope) + 1 for rank in range(1, amount + 1)]
    largest = reach if full else min(reach, max(-(-total // amount), total * portions[0] // sum(portions)))
    least = 1 if total - largest >= amount - 1 else 0
    holding, rest = [largest] + [least] * (amount - 1), total - largest - least * (amount - 1)
    while rest > 0:
        candidates = [i for i in range(1, amount) if holding[i] < largest] or [i for i in range(1, amount) if holding[i] < reach]
        pool, left = sum([portions[i] for i in candidates]), rest
        for i in candidates:
            more = min(reach - holding[i], max(1, left * portions[i] // pool), rest)
            holding[i] = holding[i] + more
            rest = rest - more
    return np.array(holding)


def gaussian(own_key, dims, width, most, pieces=(), held_as=jnp.bfloat16):
    gain = levels(own_key, dims, pieces, -0.22, 0.18) if pieces else 1.0
    array = jax.random.normal(own_key, dims, jnp.float32) * width * gain
    return jnp.minimum(jnp.maximum(array, -most), most).astype(held_as)


def setup_inputs(seed: int = 0, part: int = 0) -> dict:
    streams_of = jax.random.split(jax.random.key(seed), 6)
    part_splits = jax.random.split(jax.random.fold_in(streams_of[5], part), 6)
    routes_keys = jax.random.split(jax.random.fold_in(part_splits[0], 1), TOKENS // TOK_DEV)
    routes_turns = jax.random.permutation(jax.random.fold_in(part_splits[0], 3), TOKENS // TOK_DEV)
    routes = jax.vmap(lambda own, number: deal_out(jax.random.fold_in(part_splits[0], 2), own, number, TOK_DEV, EXPERTS, TOP, CAP, 2))(routes_keys, routes_turns).reshape((TOKENS, TOP))
    acts = draw_acts(jax.random.fold_in(jax.random.fold_in(streams_of[5], part), 71), part)
    grads = draw_grads(jax.random.fold_in(jax.random.fold_in(streams_of[5], part), 71), part)
    weights = gaussian(part_splits[3], (EXPERTS, D, F), 1.0, 6.0, ((0, 16),))
    cluster = draw_cluster(jax.random.fold_in(jax.random.fold_in(streams_of[5], part), 71), part)
    return dict(routes=routes, acts=acts, grads=grads, weights=weights, cluster=cluster)


PRIOR_WEIGHT = 1.0


def reference(routes, acts, grads, weights, cluster):
    pair_count = TOKENS * TOP
    most_rows = N_EXPERT * CAP
    flat_ids = routes.reshape(pair_count)
    sq_act = jnp.square(acts.astype(jnp.float32)).astype(jnp.bfloat16)
    sq_grad = jnp.square(grads.astype(jnp.float32)).astype(jnp.bfloat16).reshape(pair_count, F)
    counts = jax.ops.segment_sum(jnp.ones((pair_count,), jnp.int32), flat_ids, num_segments=EXPERTS)
    sorted_pairs = jnp.argsort(flat_ids, stable=True).astype(jnp.int32)
    starts = (jnp.cumsum(counts) - counts).astype(jnp.int32)
    members = jnp.argsort(cluster, stable=True).astype(jnp.int32).reshape(CLUSTERS, 2)
    lane_ids = jnp.arange(most_rows, dtype=jnp.int32)

    def fisher(expert_id):
        spot_ids = jnp.clip(starts[expert_id] + lane_ids, 0, pair_count - 1)
        row_ids = sorted_pairs[spot_ids]
        live_mask = (lane_ids < counts[expert_id]).astype(jnp.float32)
        left_side = sq_act[row_ids // TOP].astype(jnp.float32) * live_mask[:, None]
        right_side = sq_grad[row_ids].astype(jnp.float32)
        fisher_sum = lax.dot_general(left_side, right_side, (((0,), (0,)), ((), ())),
                                     precision=lax.Precision.HIGHEST, preferred_element_type=jnp.float32)
        return fisher_sum / counts[expert_id].astype(jnp.float32)

    def merge_pair(member_ids):
        first_id = member_ids[0]
        second = member_ids[1]
        prec_one = fisher(first_id) + PRIOR_WEIGHT
        prec_two = fisher(second) + PRIOR_WEIGHT
        weight_one = weights[first_id].astype(jnp.float32)
        weight_two = weights[second].astype(jnp.float32)
        return (prec_one * weight_one + prec_two * weight_two) / (prec_one + prec_two)

    return lax.map(merge_pair, members)
```

```python
import functools

import jax
import jax.numpy as jnp
from jax import lax
from jax.experimental import pallas as pl
from jax.experimental.pallas import tpu as pltpu
from jax.sharding import PartitionSpec as P

PRIOR_WEIGHT = 1.0
CHUNKS = 2
X_LAG = 2
VMEM_BYTES = 56 * 2**20
GATHER_BYTES = 32 * 2**20


def routed(routes, acts, grads, weights, cluster):
    experts = lax.axis_size("expert")
    tok_rows, fanout = routes.shape
    model_cols = acts.shape[1]
    hidden = grads.shape[2]
    pair_count = tok_rows * fanout
    slot_count = 2 * pair_count // experts
    slab_rows = model_cols // experts
    expert_ids = jnp.arange(experts, dtype=jnp.int32)
    moved_w = lax.all_to_all(
        weights.reshape(experts, slab_rows, hidden),
        "expert",
        split_axis=0,
        concat_axis=0,
        tiled=True,
    )
    flat_ids = routes.reshape(pair_count)
    onehot = (flat_ids[:, None] == expert_ids[None, :]).astype(jnp.int32)
    running = jnp.cumsum(onehot, axis=0)
    position = jnp.sum(onehot * running, axis=1) - 1
    target = flat_ids * slot_count + position
    sq_act = jnp.square(acts.astype(jnp.float32)).astype(jnp.bfloat16)
    sq_grad = jnp.square(grads.astype(jnp.float32)).astype(jnp.bfloat16).reshape(pair_count, hidden)
    pair_act = jnp.repeat(sq_act, fanout, axis=0)
    send_act = jnp.zeros((experts * slot_count, model_cols), jnp.bfloat16).at[target].set(pair_act)
    send_act = send_act.reshape(experts, slot_count, model_cols)
    send_grad = jnp.zeros((experts * slot_count, hidden), jnp.bfloat16).at[target].set(sq_grad)
    send_grad = send_grad.reshape(experts, slot_count, hidden)
    totals = lax.psum(jnp.sum(onehot, axis=0), "expert")
    own_index = lax.axis_index("expert")
    own_count = jnp.sum(jnp.where(expert_ids == own_index, totals, 0)).astype(jnp.float32)
    got_act, got_grad = (
        lax.all_to_all(send_act, "expert", split_axis=0, concat_axis=0, tiled=True),
        lax.all_to_all(send_grad, "expert", split_axis=0, concat_axis=0, tiled=True),
    )
    fisher_sum = lax.dot_general(
        got_act.reshape(experts * slot_count, model_cols),
        got_grad.reshape(experts * slot_count, hidden),
        (((0,), (0,)), ((), ())),
        preferred_element_type=jnp.float32,
    )
    precision = fisher_sum / own_count + PRIOR_WEIGHT
    member = (cluster[None, :] == jnp.arange(experts // 2, dtype=jnp.int32)[:, None]).astype(
        jnp.float32
    )
    moved_p = lax.all_to_all(
        precision.reshape(experts, slab_rows, hidden),
        "expert",
        split_axis=0,
        concat_axis=0,
        tiled=True,
    )
    scaled = moved_p * moved_w.astype(jnp.float32)
    numerator = jnp.einsum("ce,erf->crf", member, scaled, precision=lax.Precision.HIGHEST)
    denominator = jnp.einsum("ce,erf->crf", member, moved_p, precision=lax.Precision.HIGHEST)
    return numerator / denominator


def merge_kernel(
    n,
    routes_ref,
    acts_ref,
    grads_ref,
    weights_ref,
    cluster_ref,
    out_ref,
    rt_v,
    act_v,
    g_v,
    w_v,
    acc,
    lhs,
    gsq,
    rep,
    cnt,
    inv,
    rt_send,
    rt_recv,
    act_send,
    act_recv,
    w_send,
    w_recv,
    g_send,
    g_recv,
):
    nz = n // 4
    slab = act_v.shape[2]
    rows = g_v.shape[2]
    hidden = g_v.shape[3]
    fanout = rows * CHUNKS // act_v.shape[1]
    me = lax.axis_index("expert")
    core = lax.rem(me, 2)
    x = lax.rem(me // 2, 2)
    z = me // 4
    x_peer = (z * 2 + (1 - x)) * 2 + core
    sibling = (z * 2 + x) * 2 + (1 - core)

    def far(i):
        return lax.rem(me + i, n)

    barrier = pltpu.get_barrier_semaphore()

    @pl.loop(1, n)
    def _(i):
        pl.semaphore_signal(
            barrier, inc=1, device_id={"expert": far(i)}, device_id_type=pl.DeviceIdType.MESH
        )

    pl.semaphore_wait(barrier, n - 1)

    def remote(src, dst, send, recv, peer):
        return pltpu.make_async_remote_copy(
            src_ref=src,
            dst_ref=dst,
            send_sem=send,
            recv_sem=recv,
            device_id={"expert": peer},
            device_id_type=pl.DeviceIdType.MESH,
        )

    def columns(owner):
        return acts_ref.at[:, pl.ds(pl.multiple_of(owner * slab, slab), slab)]

    def weight_rows(owner):
        return weights_ref.at[pl.ds(pl.multiple_of(owner * slab, slab), slab)]

    def rt_copy(peer):
        return remote(routes_ref, rt_v.at[me], rt_send.at[peer], rt_recv.at[me], peer)

    def act_copy(peer):
        return remote(columns(peer), act_v.at[me], act_send.at[peer], act_recv.at[me], peer)

    def w_copy(peer):
        return remote(weight_rows(peer), w_v.at[me], w_send.at[peer], w_recv.at[me], peer)

    def own_rows(j):
        return grads_ref.at[pl.ds(pl.multiple_of(j * rows, rows), rows)]

    def g_copy(b, j, kind, peer):
        return remote(
            g_v.at[b, j], g_v.at[b, j], g_send.at[kind, b, j], g_recv.at[b, j], peer
        )

    def g_own_copy(j, kind, peer):
        return remote(own_rows(j), g_v.at[me, j], g_send.at[kind, me, j], g_recv.at[me, j], peer)

    def arrived(dst, sem):
        pltpu.make_async_copy(dst, dst, sem).wait()

    pltpu.make_async_copy(routes_ref, rt_v.at[me], rt_recv.at[me]).start()
    pltpu.make_async_copy(columns(me), act_v.at[me], act_recv.at[me]).start()

    @pl.loop(1, n)
    def _(i):
        rt_copy(far(i)).start()
        act_copy(far(i)).start()

    @pl.loop(0, CHUNKS)
    def _(j):
        @pl.when(z > 0)
        def _():
            g_own_copy(j, 0, me - 4).start()

        @pl.when(z < nz - 1)
        def _():
            g_own_copy(j, 1, me + 4).start()

        g_own_copy(j, 2, x_peer).start()
        g_own_copy(j, 3, sibling).start()
        pltpu.make_async_copy(own_rows(j), g_v.at[me, j], g_recv.at[me, j]).start()

    pltpu.make_async_copy(weight_rows(me), w_v.at[me], w_recv.at[me]).start()

    acc[...] = jnp.zeros_like(acc)
    cnt[...] = jnp.zeros_like(cnt)
    token = lax.broadcasted_iota(jnp.int32, (act_v.shape[1], rows), 0)
    pair = lax.broadcasted_iota(jnp.int32, (act_v.shape[1], rows), 1)
    for j in range(CHUNKS):
        rep[j] = jnp.where(token == (pair + j * rows) // fanout, 1.0, 0.0).astype(jnp.bfloat16)

    def add_block(b, j):
        grad = g_v[b, j].astype(jnp.float32)
        gsq[...] = (grad * grad).astype(jnp.bfloat16)
        act = act_v[b].astype(jnp.float32)
        sq_act = (act * act).astype(jnp.bfloat16)
        wide = lax.dot_general(
            sq_act, rep[j], (((0,), (0,)), ((), ())), preferred_element_type=jnp.float32
        ).astype(jnp.bfloat16)
        named = rt_v[b, j]
        ids = lax.broadcasted_iota(jnp.int32, (n, rows), 0)
        mask = jnp.where(ids == named, 1.0, 0.0)
        cnt[...] += mask
        for e in range(n):
            keep = jnp.broadcast_to(mask[e : e + 1].astype(jnp.bfloat16), (slab, rows))
            lhs[e * slab : (e + 1) * slab, :] = wide * keep
        step = 256 if hidden % 256 == 0 else hidden
        for k in range(0, hidden, step):
            acc[:, :, k : k + step] += jnp.dot(
                lhs[...], gsq[:, k : k + step], preferred_element_type=jnp.float32
            ).reshape(n, slab, step)

    turns = (nz + X_LAG) * CHUNKS
    burst = -(-(n - 1) // (turns // 2))

    @pl.loop(0, turns)
    def _(turn):
        r = turn // CHUNKS
        j = lax.rem(turn, CHUNKS)
        for k in range(burst):
            i = turn * burst + k + 1

            @pl.when(i < n)
            def _(i=i):
                w_copy(far(i)).start()

        @pl.loop(0, 8)
        def _(q):
            other_core = q // 4
            other_x = lax.rem(q // 2, 2)
            up = lax.rem(q, 2)
            dist = r - X_LAG * other_x
            z0 = z + (2 * up - 1) * dist
            b = (z0 * 2 + lax.rem(x + other_x, 2)) * 2 + lax.rem(core + other_core, 2)
            inside = (dist >= 0) & (dist < nz) & (z0 >= 0) & (z0 < nz)

            @pl.when(inside & ((dist > 0) | (up == 0)))
            def _():
                arrived(g_v.at[b, j], g_recv.at[b, j])

                @pl.when((other_core == 0) & (b != me))
                def _():
                    @pl.when(other_x == 0)
                    def _():
                        @pl.when((up == 1) & (z > 0))
                        def _():
                            g_copy(b, j, 0, me - 4).start()

                        @pl.when((up == 0) & (z < nz - 1))
                        def _():
                            g_copy(b, j, 1, me + 4).start()

                        g_copy(b, j, 2, x_peer).start()

                    g_copy(b, j, 3, sibling).start()

                @pl.when(j == 0)
                def _():
                    arrived(rt_v.at[b], rt_recv.at[b])
                    arrived(act_v.at[b], act_recv.at[b])

                add_block(b, j)

    share = 1.0 / jnp.sum(cnt[...], axis=1, keepdims=True)
    for e in range(n):
        inv[e] = jnp.broadcast_to(share[e : e + 1], inv.shape[1:])

    @pl.loop(0, n)
    def _(e):
        arrived(w_v.at[e], w_recv.at[e])

    @pl.loop(0, n // 2)
    def _(c):
        first = jnp.int32(n - 1)
        second = jnp.int32(0)
        for e in range(n):
            hit = cluster_ref[e] == c
            first = jnp.where(hit, jnp.minimum(first, e), first)
            second = jnp.where(hit, jnp.maximum(second, e), second)
        p_one = acc[first] * inv[first][:1, :1] + PRIOR_WEIGHT
        p_two = acc[second] * inv[second][:1, :1] + PRIOR_WEIGHT
        w_one = w_v[first].astype(jnp.float32)
        w_two = w_v[second].astype(jnp.float32)
        out_ref[c] = (p_one * w_one + p_two * w_two) / (p_one + p_two)

    @pl.loop(1, n)
    def _(i):
        rt_copy(far(i)).wait_send()
        act_copy(far(i)).wait_send()
        w_copy(far(i)).wait_send()

    @pl.loop(0, n * CHUNKS)
    def _(s):
        b = s // CHUNKS
        j = lax.rem(s, CHUNKS)
        z0 = b // 4
        same_core = lax.rem(b, 2) == core
        same_column = same_core & (lax.rem(b // 2, 2) == x)

        @pl.when(same_column & (z0 >= z) & (z > 0))
        def _():
            g_copy(b, j, 0, me - 4).wait_send()

        @pl.when(same_column & (z0 <= z) & (z < nz - 1))
        def _():
            g_copy(b, j, 1, me + 4).wait_send()

        @pl.when(same_column)
        def _():
            g_copy(b, j, 2, x_peer).wait_send()

        @pl.when(same_core)
        def _():
            g_copy(b, j, 3, sibling).wait_send()


def gathered(routes, acts, grads, weights, cluster):
    n = lax.axis_size("expert")
    tok_rows, fanout = routes.shape
    hidden = grads.shape[2]
    slab = acts.shape[1] // n
    pairs = tok_rows * fanout
    rows = pairs // CHUNKS
    anywhere = pl.BlockSpec(memory_space=pl.ANY)
    dma = pltpu.SemaphoreType.DMA
    bf16 = jnp.bfloat16
    return pl.pallas_call(
        functools.partial(merge_kernel, n),
        out_shape=jax.ShapeDtypeStruct((n // 2, slab, hidden), jnp.float32),
        in_specs=[anywhere] * 4 + [pl.BlockSpec(memory_space=pltpu.SMEM)],
        out_specs=pl.BlockSpec(memory_space=pltpu.VMEM),
        scratch_shapes=[
            pltpu.VMEM((n, CHUNKS, 1, rows), jnp.int32),
            pltpu.VMEM((n, tok_rows, slab), bf16),
            pltpu.VMEM((n, CHUNKS, rows, hidden), bf16),
            pltpu.VMEM((n, slab, hidden), bf16),
            pltpu.VMEM((n, slab, hidden), jnp.float32),
            pltpu.VMEM((n * slab, rows), bf16),
            pltpu.VMEM((rows, hidden), bf16),
            pltpu.VMEM((CHUNKS, tok_rows, rows), bf16),
            pltpu.VMEM((n, rows), jnp.float32),
            pltpu.VMEM((n, 8, 128), jnp.float32),
            dma((n,)),
            dma((n,)),
            dma((n,)),
            dma((n,)),
            dma((n,)),
            dma((n,)),
            dma((4, n, CHUNKS)),
            dma((n, CHUNKS)),
        ],
        compiler_params=pltpu.CompilerParams(
            collective_id=0, has_side_effects=True, vmem_limit_bytes=VMEM_BYTES
        ),
        cost_estimate=pl.CostEstimate(
            flops=2 * n * pairs * n * slab * hidden,
            bytes_accessed=2 * n * pairs * hidden,
            transcendentals=0,
        ),
    )(
        routes.reshape(CHUNKS, 1, rows),
        acts,
        grads.reshape(pairs, hidden),
        weights.reshape(n * slab, hidden),
        cluster,
    )


def on_device(routes, acts, grads, weights, cluster):
    n = lax.axis_size("expert")
    if n % 4 or 2 * n * grads.size > GATHER_BYTES:
        return routed(routes, acts, grads, weights, cluster)
    return gathered(routes, acts, grads, weights, cluster)


def solution(mesh):
    return jax.shard_map(
        on_device,
        mesh=mesh,
        in_specs=(
            P(("groups", "expert"), None),
            P(("groups", "expert"), None),
            P(("groups", "expert"), None, None),
            P(("groups", "expert"), None, None),
            P("groups"),
        ),
        out_specs=P("groups", "expert", None),
        check_vma=False,
    )
```

```python
import functools

import jax
import jax.numpy as jnp
from jax import lax
from jax.experimental import pallas as pl
from jax.experimental.pallas import tpu as pltpu
from jax.sharding import PartitionSpec as P

PRIOR_WEIGHT = 1.0
CHUNKS = 4
JOINED = 2
X_LAG = 1
VMEM_BYTES = 56 * 2**20
GATHER_BYTES = 32 * 2**20


def routed(routes, acts, grads, weights, cluster):
    experts = lax.axis_size("expert")
    tok_rows, fanout = routes.shape
    model_cols = acts.shape[1]
    hidden = grads.shape[2]
    pair_count = tok_rows * fanout
    slot_count = 2 * pair_count // experts
    slab_rows = model_cols // experts
    expert_ids = jnp.arange(experts, dtype=jnp.int32)
    moved_w = lax.all_to_all(
        weights.reshape(experts, slab_rows, hidden),
        "expert",
        split_axis=0,
        concat_axis=0,
        tiled=True,
    )
    flat_ids = routes.reshape(pair_count)
    onehot = (flat_ids[:, None] == expert_ids[None, :]).astype(jnp.int32)
    running = jnp.cumsum(onehot, axis=0)
    position = jnp.sum(onehot * running, axis=1) - 1
    target = flat_ids * slot_count + position
    sq_act = jnp.square(acts.astype(jnp.float32)).astype(jnp.bfloat16)
    sq_grad = jnp.square(grads.astype(jnp.float32)).astype(jnp.bfloat16).reshape(pair_count, hidden)
    pair_act = jnp.repeat(sq_act, fanout, axis=0)
    send_act = jnp.zeros((experts * slot_count, model_cols), jnp.bfloat16).at[target].set(pair_act)
    send_act = send_act.reshape(experts, slot_count, model_cols)
    send_grad = jnp.zeros((experts * slot_count, hidden), jnp.bfloat16).at[target].set(sq_grad)
    send_grad = send_grad.reshape(experts, slot_count, hidden)
    totals = lax.psum(jnp.sum(onehot, axis=0), "expert")
    own_index = lax.axis_index("expert")
    own_count = jnp.sum(jnp.where(expert_ids == own_index, totals, 0)).astype(jnp.float32)
    got_act, got_grad = (
        lax.all_to_all(send_act, "expert", split_axis=0, concat_axis=0, tiled=True),
        lax.all_to_all(send_grad, "expert", split_axis=0, concat_axis=0, tiled=True),
    )
    fisher_sum = lax.dot_general(
        got_act.reshape(experts * slot_count, model_cols),
        got_grad.reshape(experts * slot_count, hidden),
        (((0,), (0,)), ((), ())),
        preferred_element_type=jnp.float32,
    )
    precision = fisher_sum / own_count + PRIOR_WEIGHT
    member = (cluster[None, :] == jnp.arange(experts // 2, dtype=jnp.int32)[:, None]).astype(
        jnp.float32
    )
    moved_p = lax.all_to_all(
        precision.reshape(experts, slab_rows, hidden),
        "expert",
        split_axis=0,
        concat_axis=0,
        tiled=True,
    )
    scaled = moved_p * moved_w.astype(jnp.float32)
    numerator = jnp.einsum("ce,erf->crf", member, scaled, precision=lax.Precision.HIGHEST)
    denominator = jnp.einsum("ce,erf->crf", member, moved_p, precision=lax.Precision.HIGHEST)
    return numerator / denominator


def merge_kernel(
    n,
    routes_ref,
    acts_ref,
    grads_ref,
    weights_ref,
    cluster_ref,
    out_ref,
    rt_v,
    act_v,
    g_v,
    w_v,
    acc,
    lhs,
    gsq,
    rep,
    cnt,
    inv,
    rt_send,
    rt_recv,
    act_send,
    act_recv,
    w_send,
    w_recv,
    g_send,
    g_recv,
):
    nz = n // 4
    slab = act_v.shape[2]
    rows = g_v.shape[2]
    span = rows * JOINED
    hidden = g_v.shape[3]
    fanout = rows * CHUNKS // act_v.shape[1]
    me = lax.axis_index("expert")
    core = lax.rem(me, 2)
    x = lax.rem(me // 2, 2)
    z = me // 4
    x_peer = (z * 2 + (1 - x)) * 2 + core
    sibling = (z * 2 + x) * 2 + (1 - core)

    def far(i):
        return lax.rem(me + i, n)

    barrier = pltpu.get_barrier_semaphore()

    @pl.loop(1, n)
    def _(i):
        pl.semaphore_signal(
            barrier, inc=1, device_id={"expert": far(i)}, device_id_type=pl.DeviceIdType.MESH
        )

    pl.semaphore_wait(barrier, n - 1)

    def remote(src, dst, send, recv, peer):
        return pltpu.make_async_remote_copy(
            src_ref=src,
            dst_ref=dst,
            send_sem=send,
            recv_sem=recv,
            device_id={"expert": peer},
            device_id_type=pl.DeviceIdType.MESH,
        )

    def columns(owner):
        return acts_ref.at[:, pl.ds(pl.multiple_of(owner * slab, slab), slab)]

    def weight_rows(owner):
        return weights_ref.at[pl.ds(pl.multiple_of(owner * slab, slab), slab)]

    def rt_copy(peer):
        return remote(routes_ref, rt_v.at[me], rt_send.at[peer], rt_recv.at[me], peer)

    def act_copy(peer):
        return remote(columns(peer), act_v.at[me], act_send.at[peer], act_recv.at[me], peer)

    def w_copy(peer):
        return remote(weight_rows(peer), w_v.at[me], w_send.at[peer], w_recv.at[me], peer)

    def own_rows(j):
        return grads_ref.at[pl.ds(pl.multiple_of(j * rows, rows), rows)]

    def g_copy(b, j, kind, peer):
        return remote(
            g_v.at[b, j], g_v.at[b, j], g_send.at[kind, b, j], g_recv.at[b, j], peer
        )

    def g_own_copy(j, kind, peer):
        return remote(own_rows(j), g_v.at[me, j], g_send.at[kind, me, j], g_recv.at[me, j], peer)

    def arrived(dst, sem):
        pltpu.make_async_copy(dst, dst, sem).wait()

    pltpu.make_async_copy(routes_ref, rt_v.at[me], rt_recv.at[me]).start()
    pltpu.make_async_copy(columns(me), act_v.at[me], act_recv.at[me]).start()

    @pl.loop(1, n)
    def _(i):
        rt_copy(far(i)).start()
        act_copy(far(i)).start()

    @pl.loop(0, CHUNKS)
    def _(j):
        @pl.when(z > 0)
        def _():
            g_own_copy(j, 0, me - 4).start()

        @pl.when(z < nz - 1)
        def _():
            g_own_copy(j, 1, me + 4).start()

        g_own_copy(j, 2, x_peer).start()
        g_own_copy(j, 3, sibling).start()
        pltpu.make_async_copy(own_rows(j), g_v.at[me, j], g_recv.at[me, j]).start()

    pltpu.make_async_copy(weight_rows(me), w_v.at[me], w_recv.at[me]).start()

    acc[...] = jnp.zeros_like(acc)
    cnt[...] = jnp.zeros_like(cnt)
    token = lax.broadcasted_iota(jnp.int32, (act_v.shape[1], span), 0)
    pair = lax.broadcasted_iota(jnp.int32, (act_v.shape[1], span), 1)
    for h in range(CHUNKS // JOINED):
        rep[h] = jnp.where(token == (pair + h * span) // fanout, 1.0, 0.0).astype(jnp.bfloat16)

    def add_block(b, h):
        grad = g_v[b, pl.ds(h * JOINED, JOINED)].reshape(span, hidden).astype(jnp.float32)
        gsq[...] = (grad * grad).astype(jnp.bfloat16)
        act = act_v[b].astype(jnp.float32)
        sq_act = (act * act).astype(jnp.bfloat16)
        wide = lax.dot_general(
            sq_act, rep[h], (((0,), (0,)), ((), ())), preferred_element_type=jnp.float32
        ).astype(jnp.bfloat16)
        named = rt_v[b, h]
        ids = lax.broadcasted_iota(jnp.int32, (n, span), 0)
        mask = jnp.where(ids == named, 1.0, 0.0)
        cnt[...] += mask
        for e in range(n):
            keep = jnp.broadcast_to(mask[e : e + 1].astype(jnp.bfloat16), (slab, span))
            lhs[e * slab : (e + 1) * slab, :] = wide * keep
        step = 256 if hidden % 256 == 0 else hidden
        for k in range(0, hidden, step):
            acc[:, :, k : k + step] += jnp.dot(
                lhs[...], gsq[:, k : k + step], preferred_element_type=jnp.float32
            ).reshape(n, slab, step)

    turns = (nz + X_LAG) * CHUNKS
    burst = -(-(n - 1) // (turns // 2))

    def place(turn, q):
        other_x = q // 2
        up = lax.rem(q, 2)
        j = lax.rem(turn, CHUNKS)
        dist = turn // CHUNKS - X_LAG * other_x
        z0 = z + (2 * up - 1) * dist
        inside = (dist >= 0) & (dist < nz) & (z0 >= 0) & (z0 < nz)
        column = z0 * 2 + lax.rem(x + other_x, 2)
        return other_x, up, dist, j, column * 2, inside & ((dist > 0) | (up == 0))

    def pass_on(turn, q):
        other_x, up, dist, j, first, live = place(turn, q)
        b = first + core

        @pl.when(live)
        def _():
            arrived(g_v.at[b, j], g_recv.at[b, j])

            @pl.when(b != me)
            def _():
                @pl.when((other_x == 0) & (up == 1) & (z > 0))
                def _():
                    g_copy(b, j, 0, me - 4).start()

                @pl.when((other_x == 0) & (up == 0) & (z < nz - 1))
                def _():
                    g_copy(b, j, 1, me + 4).start()

                @pl.when(other_x == 0)
                def _():
                    g_copy(b, j, 2, x_peer).start()

                g_copy(b, j, 3, sibling).start()

    def take(turn, q, other_core):
        _, _, _, j, first, live = place(turn, q)
        b = first + lax.rem(core + other_core, 2)

        @pl.when(live)
        def _():
            @pl.when(other_core == 1)
            def _():
                arrived(g_v.at[b, j], g_recv.at[b, j])

            @pl.when(j == 0)
            def _():
                arrived(rt_v.at[b], rt_recv.at[b])
                arrived(act_v.at[b], act_recv.at[b])

            @pl.when(lax.rem(j, JOINED) == JOINED - 1)
            def _():
                add_block(b, j // JOINED)

    @pl.loop(0, turns + 1)
    def _(turn):
        for k in range(burst):
            i = turn * burst + k + 1

            @pl.when(i < n)
            def _(i=i):
                w_copy(far(i)).start()

        @pl.loop(0, 4)
        def _(q):
            @pl.when(turn < turns)
            def _():
                pass_on(turn, q)

            @pl.when(turn > 0)
            def _():
                @pl.loop(0, 2)
                def _(other_core):
                    take(turn - 1, q, other_core)

    share = 1.0 / jnp.sum(cnt[...], axis=1, keepdims=True)
    for e in range(n):
        inv[e] = jnp.broadcast_to(share[e : e + 1], inv.shape[1:])

    @pl.loop(0, n)
    def _(e):
        arrived(w_v.at[e], w_recv.at[e])

    @pl.loop(0, n // 2)
    def _(c):
        first = jnp.int32(n - 1)
        second = jnp.int32(0)
        for e in range(n):
            hit = cluster_ref[e] == c
            first = jnp.where(hit, jnp.minimum(first, e), first)
            second = jnp.where(hit, jnp.maximum(second, e), second)
        p_one = acc[first] * inv[first][:1, :1] + PRIOR_WEIGHT
        p_two = acc[second] * inv[second][:1, :1] + PRIOR_WEIGHT
        w_one = w_v[first].astype(jnp.float32)
        w_two = w_v[second].astype(jnp.float32)
        out_ref[c] = (p_one * w_one + p_two * w_two) / (p_one + p_two)

    @pl.loop(1, n)
    def _(i):
        rt_copy(far(i)).wait_send()
        act_copy(far(i)).wait_send()
        w_copy(far(i)).wait_send()

    @pl.loop(0, n * CHUNKS)
    def _(s):
        b = s // CHUNKS
        j = lax.rem(s, CHUNKS)
        z0 = b // 4
        same_core = lax.rem(b, 2) == core
        same_column = same_core & (lax.rem(b // 2, 2) == x)

        @pl.when(same_column & (z0 >= z) & (z > 0))
        def _():
            g_copy(b, j, 0, me - 4).wait_send()

        @pl.when(same_column & (z0 <= z) & (z < nz - 1))
        def _():
            g_copy(b, j, 1, me + 4).wait_send()

        @pl.when(same_column)
        def _():
            g_copy(b, j, 2, x_peer).wait_send()

        @pl.when(same_core)
        def _():
            g_copy(b, j, 3, sibling).wait_send()


def gathered(routes, acts, grads, weights, cluster):
    n = lax.axis_size("expert")
    tok_rows, fanout = routes.shape
    hidden = grads.shape[2]
    slab = acts.shape[1] // n
    pairs = tok_rows * fanout
    rows = pairs // CHUNKS
    span = rows * JOINED
    anywhere = pl.BlockSpec(memory_space=pl.ANY)
    dma = pltpu.SemaphoreType.DMA
    bf16 = jnp.bfloat16
    return pl.pallas_call(
        functools.partial(merge_kernel, n),
        out_shape=jax.ShapeDtypeStruct((n // 2, slab, hidden), jnp.float32),
        in_specs=[anywhere] * 4 + [pl.BlockSpec(memory_space=pltpu.SMEM)],
        out_specs=pl.BlockSpec(memory_space=pltpu.VMEM),
        scratch_shapes=[
            pltpu.VMEM((n, CHUNKS // JOINED, 1, span), jnp.int32),
            pltpu.VMEM((n, tok_rows, slab), bf16),
            pltpu.VMEM((n, CHUNKS, rows, hidden), bf16),
            pltpu.VMEM((n, slab, hidden), bf16),
            pltpu.VMEM((n, slab, hidden), jnp.float32),
            pltpu.VMEM((n * slab, span), bf16),
            pltpu.VMEM((span, hidden), bf16),
            pltpu.VMEM((CHUNKS // JOINED, tok_rows, span), bf16),
            pltpu.VMEM((n, span), jnp.float32),
            pltpu.VMEM((n, 8, 128), jnp.float32),
            dma((n,)),
            dma((n,)),
            dma((n,)),
            dma((n,)),
            dma((n,)),
            dma((n,)),
            dma((4, n, CHUNKS)),
            dma((n, CHUNKS)),
        ],
        compiler_params=pltpu.CompilerParams(
            collective_id=0, has_side_effects=True, vmem_limit_bytes=VMEM_BYTES
        ),
        cost_estimate=pl.CostEstimate(
            flops=2 * n * pairs * n * slab * hidden,
            bytes_accessed=2 * n * pairs * hidden,
            transcendentals=0,
        ),
    )(
        routes.reshape(CHUNKS // JOINED, 1, span),
        acts,
        grads.reshape(pairs, hidden),
        weights.reshape(n * slab, hidden),
        cluster,
    )


def on_device(routes, acts, grads, weights, cluster):
    n = lax.axis_size("expert")
    if n % 4 or 2 * n * grads.size > GATHER_BYTES:
        return routed(routes, acts, grads, weights, cluster)
    return gathered(routes, acts, grads, weights, cluster)


def solution(mesh):
    return jax.shard_map(
        on_device,
        mesh=mesh,
        in_specs=(
            P(("groups", "expert"), None),
            P(("groups", "expert"), None),
            P(("groups", "expert"), None, None),
            P(("groups", "expert"), None, None),
            P("groups"),
        ),
        out_specs=P("groups", "expert", None),
        check_vma=False,
    )
```

```python
import functools

import jax
import jax.numpy as jnp
from jax import lax
from jax.experimental import pallas as pl
from jax.experimental.pallas import tpu as pltpu
from jax.sharding import PartitionSpec as P

PRIOR_WEIGHT = 1.0
CHUNKS = 4
JOINED = 1
X_LAG = 1
VMEM_BYTES = 56 * 2**20
GATHER_BYTES = 32 * 2**20


def routed(routes, acts, grads, weights, cluster):
    experts = lax.axis_size("expert")
    tok_rows, fanout = routes.shape
    model_cols = acts.shape[1]
    hidden = grads.shape[2]
    pair_count = tok_rows * fanout
    slot_count = 2 * pair_count // experts
    slab_rows = model_cols // experts
    expert_ids = jnp.arange(experts, dtype=jnp.int32)
    moved_w = lax.all_to_all(
        weights.reshape(experts, slab_rows, hidden),
        "expert",
        split_axis=0,
        concat_axis=0,
        tiled=True,
    )
    flat_ids = routes.reshape(pair_count)
    onehot = (flat_ids[:, None] == expert_ids[None, :]).astype(jnp.int32)
    running = jnp.cumsum(onehot, axis=0)
    position = jnp.sum(onehot * running, axis=1) - 1
    target = flat_ids * slot_count + position
    sq_act = jnp.square(acts.astype(jnp.float32)).astype(jnp.bfloat16)
    sq_grad = jnp.square(grads.astype(jnp.float32)).astype(jnp.bfloat16).reshape(pair_count, hidden)
    pair_act = jnp.repeat(sq_act, fanout, axis=0)
    send_act = jnp.zeros((experts * slot_count, model_cols), jnp.bfloat16).at[target].set(pair_act)
    send_act = send_act.reshape(experts, slot_count, model_cols)
    send_grad = jnp.zeros((experts * slot_count, hidden), jnp.bfloat16).at[target].set(sq_grad)
    send_grad = send_grad.reshape(experts, slot_count, hidden)
    totals = lax.psum(jnp.sum(onehot, axis=0), "expert")
    own_index = lax.axis_index("expert")
    own_count = jnp.sum(jnp.where(expert_ids == own_index, totals, 0)).astype(jnp.float32)
    got_act, got_grad = (
        lax.all_to_all(send_act, "expert", split_axis=0, concat_axis=0, tiled=True),
        lax.all_to_all(send_grad, "expert", split_axis=0, concat_axis=0, tiled=True),
    )
    fisher_sum = lax.dot_general(
        got_act.reshape(experts * slot_count, model_cols),
        got_grad.reshape(experts * slot_count, hidden),
        (((0,), (0,)), ((), ())),
        preferred_element_type=jnp.float32,
    )
    precision = fisher_sum / own_count + PRIOR_WEIGHT
    member = (cluster[None, :] == jnp.arange(experts // 2, dtype=jnp.int32)[:, None]).astype(
        jnp.float32
    )
    moved_p = lax.all_to_all(
        precision.reshape(experts, slab_rows, hidden),
        "expert",
        split_axis=0,
        concat_axis=0,
        tiled=True,
    )
    scaled = moved_p * moved_w.astype(jnp.float32)
    numerator = jnp.einsum("ce,erf->crf", member, scaled, precision=lax.Precision.HIGHEST)
    denominator = jnp.einsum("ce,erf->crf", member, moved_p, precision=lax.Precision.HIGHEST)
    return numerator / denominator


def merge_kernel(
    n,
    routes_ref,
    acts_ref,
    grads_ref,
    weights_ref,
    cluster_ref,
    out_ref,
    rt_v,
    act_v,
    g_v,
    w_v,
    acc,
    lhs,
    gsq,
    rep,
    cnt,
    inv,
    rt_send,
    rt_recv,
    act_send,
    act_recv,
    w_send,
    w_recv,
    g_send,
    g_recv,
):
    nz = n // 4
    slab = act_v.shape[2]
    rows = g_v.shape[2]
    span = rows * JOINED
    hidden = g_v.shape[3]
    fanout = rows * CHUNKS // act_v.shape[1]
    me = lax.axis_index("expert")
    core = lax.rem(me, 2)
    x = lax.rem(me // 2, 2)
    z = me // 4
    x_peer = (z * 2 + (1 - x)) * 2 + core
    sibling = (z * 2 + x) * 2 + (1 - core)

    def far(i):
        return lax.rem(me + i, n)

    barrier = pltpu.get_barrier_semaphore()

    @pl.loop(1, n)
    def _(i):
        pl.semaphore_signal(
            barrier, inc=1, device_id={"expert": far(i)}, device_id_type=pl.DeviceIdType.MESH
        )

    pl.semaphore_wait(barrier, n - 1)

    def remote(src, dst, send, recv, peer):
        return pltpu.make_async_remote_copy(
            src_ref=src,
            dst_ref=dst,
            send_sem=send,
            recv_sem=recv,
            device_id={"expert": peer},
            device_id_type=pl.DeviceIdType.MESH,
        )

    def columns(owner):
        return acts_ref.at[:, pl.ds(pl.multiple_of(owner * slab, slab), slab)]

    def weight_rows(owner):
        return weights_ref.at[pl.ds(pl.multiple_of(owner * slab, slab), slab)]

    def rt_copy(peer):
        return remote(routes_ref, rt_v.at[me], rt_send.at[peer], rt_recv.at[me], peer)

    def act_copy(peer):
        return remote(columns(peer), act_v.at[me], act_send.at[peer], act_recv.at[me], peer)

    def w_copy(peer):
        return remote(weight_rows(peer), w_v.at[me], w_send.at[peer], w_recv.at[me], peer)

    def own_rows(j):
        return grads_ref.at[pl.ds(pl.multiple_of(j * rows, rows), rows)]

    def g_copy(b, j, kind, peer):
        return remote(
            g_v.at[b, j], g_v.at[b, j], g_send.at[kind, b, j], g_recv.at[b, j], peer
        )

    def g_own_copy(j, kind, peer):
        return remote(own_rows(j), g_v.at[me, j], g_send.at[kind, me, j], g_recv.at[me, j], peer)

    def arrived(dst, sem):
        pltpu.make_async_copy(dst, dst, sem).wait()

    pltpu.make_async_copy(routes_ref, rt_v.at[me], rt_recv.at[me]).start()
    pltpu.make_async_copy(columns(me), act_v.at[me], act_recv.at[me]).start()

    @pl.loop(1, n)
    def _(i):
        rt_copy(far(i)).start()
        act_copy(far(i)).start()

    @pl.loop(0, CHUNKS)
    def _(j):
        @pl.when(z > 0)
        def _():
            g_own_copy(j, 0, me - 4).start()

        @pl.when(z < nz - 1)
        def _():
            g_own_copy(j, 1, me + 4).start()

        g_own_copy(j, 2, x_peer).start()
        g_own_copy(j, 3, sibling).start()
        pltpu.make_async_copy(own_rows(j), g_v.at[me, j], g_recv.at[me, j]).start()

    pltpu.make_async_copy(weight_rows(me), w_v.at[me], w_recv.at[me]).start()

    acc[...] = jnp.zeros_like(acc)
    cnt[...] = jnp.zeros_like(cnt)
    token = lax.broadcasted_iota(jnp.int32, (act_v.shape[1], span), 0)
    pair = lax.broadcasted_iota(jnp.int32, (act_v.shape[1], span), 1)
    for h in range(CHUNKS // JOINED):
        rep[h] = jnp.where(token == (pair + h * span) // fanout, 1.0, 0.0).astype(jnp.bfloat16)

    def add_block(b, h):
        grad = g_v[b, pl.ds(h * JOINED, JOINED)].reshape(span, hidden).astype(jnp.float32)
        gsq[...] = (grad * grad).astype(jnp.bfloat16)
        act = act_v[b].astype(jnp.float32)
        sq_act = (act * act).astype(jnp.bfloat16)
        wide = lax.dot_general(
            sq_act, rep[h], (((0,), (0,)), ((), ())), preferred_element_type=jnp.float32
        ).astype(jnp.bfloat16)
        named = rt_v[b, h]
        ids = lax.broadcasted_iota(jnp.int32, (n, span), 0)
        mask = jnp.where(ids == named, 1.0, 0.0)
        cnt[...] += mask
        for e in range(n):
            keep = jnp.broadcast_to(mask[e : e + 1].astype(jnp.bfloat16), (slab, span))
            lhs[e * slab : (e + 1) * slab, :] = wide * keep
        step = 256 if hidden % 256 == 0 else hidden
        for k in range(0, hidden, step):
            acc[:, :, k : k + step] += jnp.dot(
                lhs[...], gsq[:, k : k + step], preferred_element_type=jnp.float32
            ).reshape(n, slab, step)

    turns = (nz + X_LAG) * CHUNKS
    burst = -(-(n - 1) // (turns // 2))

    def place(turn, q):
        other_x = q // 2
        up = lax.rem(q, 2)
        j = lax.rem(turn, CHUNKS)
        dist = turn // CHUNKS - X_LAG * other_x
        z0 = z + (2 * up - 1) * dist
        inside = (dist >= 0) & (dist < nz) & (z0 >= 0) & (z0 < nz)
        column = z0 * 2 + lax.rem(x + other_x, 2)
        return other_x, up, dist, j, column * 2, inside & ((dist > 0) | (up == 0))

    def pass_on(turn, q):
        other_x, up, dist, j, first, live = place(turn, q)
        b = first + core

        @pl.when(live)
        def _():
            arrived(g_v.at[b, j], g_recv.at[b, j])

            @pl.when(b != me)
            def _():
                @pl.when((other_x == 0) & (up == 1) & (z > 0))
                def _():
                    g_copy(b, j, 0, me - 4).start()

                @pl.when((other_x == 0) & (up == 0) & (z < nz - 1))
                def _():
                    g_copy(b, j, 1, me + 4).start()

                @pl.when(other_x == 0)
                def _():
                    g_copy(b, j, 2, x_peer).start()

                g_copy(b, j, 3, sibling).start()

    def take(turn, q, other_core):
        _, _, _, j, first, live = place(turn, q)
        b = first + lax.rem(core + other_core, 2)

        @pl.when(live)
        def _():
            @pl.when(other_core == 1)
            def _():
                arrived(g_v.at[b, j], g_recv.at[b, j])

            @pl.when(j == 0)
            def _():
                arrived(rt_v.at[b], rt_recv.at[b])
                arrived(act_v.at[b], act_recv.at[b])

            @pl.when(lax.rem(j, JOINED) == JOINED - 1)
            def _():
                add_block(b, j // JOINED)

    @pl.loop(0, turns + 1)
    def _(turn):
        for k in range(burst):
            i = turn * burst + k + 1

            @pl.when(i < n)
            def _(i=i):
                w_copy(far(i)).start()

        @pl.loop(0, 4)
        def _(q):
            @pl.when(turn < turns)
            def _():
                pass_on(turn, q)

            @pl.when(turn > 0)
            def _():
                @pl.loop(0, 2)
                def _(other_core):
                    take(turn - 1, q, other_core)

    share = 1.0 / jnp.sum(cnt[...], axis=1, keepdims=True)
    for e in range(n):
        inv[e] = jnp.broadcast_to(share[e : e + 1], inv.shape[1:])

    @pl.loop(0, n)
    def _(e):
        arrived(w_v.at[e], w_recv.at[e])

    @pl.loop(0, n // 2)
    def _(c):
        first = jnp.int32(n - 1)
        second = jnp.int32(0)
        for e in range(n):
            hit = cluster_ref[e] == c
            first = jnp.where(hit, jnp.minimum(first, e), first)
            second = jnp.where(hit, jnp.maximum(second, e), second)
        p_one = acc[first] * inv[first][:1, :1] + PRIOR_WEIGHT
        p_two = acc[second] * inv[second][:1, :1] + PRIOR_WEIGHT
        w_one = w_v[first].astype(jnp.float32)
        w_two = w_v[second].astype(jnp.float32)
        out_ref[c] = (p_one * w_one + p_two * w_two) / (p_one + p_two)

    @pl.loop(1, n)
    def _(i):
        rt_copy(far(i)).wait_send()
        act_copy(far(i)).wait_send()
        w_copy(far(i)).wait_send()

    @pl.loop(0, n * CHUNKS)
    def _(s):
        b = s // CHUNKS
        j = lax.rem(s, CHUNKS)
        z0 = b // 4
        same_core = lax.rem(b, 2) == core
        same_column = same_core & (lax.rem(b // 2, 2) == x)

        @pl.when(same_column & (z0 >= z) & (z > 0))
        def _():
            g_copy(b, j, 0, me - 4).wait_send()

        @pl.when(same_column & (z0 <= z) & (z < nz - 1))
        def _():
            g_copy(b, j, 1, me + 4).wait_send()

        @pl.when(same_column)
        def _():
            g_copy(b, j, 2, x_peer).wait_send()

        @pl.when(same_core)
        def _():
            g_copy(b, j, 3, sibling).wait_send()


def gathered(routes, acts, grads, weights, cluster):
    n = lax.axis_size("expert")
    tok_rows, fanout = routes.shape
    hidden = grads.shape[2]
    slab = acts.shape[1] // n
    pairs = tok_rows * fanout
    rows = pairs // CHUNKS
    span = rows * JOINED
    anywhere = pl.BlockSpec(memory_space=pl.ANY)
    dma = pltpu.SemaphoreType.DMA
    bf16 = jnp.bfloat16
    return pl.pallas_call(
        functools.partial(merge_kernel, n),
        out_shape=jax.ShapeDtypeStruct((n // 2, slab, hidden), jnp.float32),
        in_specs=[anywhere] * 4 + [pl.BlockSpec(memory_space=pltpu.SMEM)],
        out_specs=pl.BlockSpec(memory_space=pltpu.VMEM),
        scratch_shapes=[
            pltpu.VMEM((n, CHUNKS // JOINED, 1, span), jnp.int32),
            pltpu.VMEM((n, tok_rows, slab), bf16),
            pltpu.VMEM((n, CHUNKS, rows, hidden), bf16),
            pltpu.VMEM((n, slab, hidden), bf16),
            pltpu.VMEM((n, slab, hidden), jnp.float32),
            pltpu.VMEM((n * slab, span), bf16),
            pltpu.VMEM((span, hidden), bf16),
            pltpu.VMEM((CHUNKS // JOINED, tok_rows, span), bf16),
            pltpu.VMEM((n, span), jnp.float32),
            pltpu.VMEM((n, 8, 128), jnp.float32),
            dma((n,)),
            dma((n,)),
            dma((n,)),
            dma((n,)),
            dma((n,)),
            dma((n,)),
            dma((4, n, CHUNKS)),
            dma((n, CHUNKS)),
        ],
        compiler_params=pltpu.CompilerParams(
            collective_id=0, has_side_effects=True, vmem_limit_bytes=VMEM_BYTES
        ),
        cost_estimate=pl.CostEstimate(
            flops=2 * n * pairs * n * slab * hidden,
            bytes_accessed=2 * n * pairs * hidden,
            transcendentals=0,
        ),
    )(
        routes.reshape(CHUNKS // JOINED, 1, span),
        acts,
        grads.reshape(pairs, hidden),
        weights.reshape(n * slab, hidden),
        cluster,
    )


def on_device(routes, acts, grads, weights, cluster):
    n = lax.axis_size("expert")
    if n % 4 or 2 * n * grads.size > GATHER_BYTES:
        return routed(routes, acts, grads, weights, cluster)
    return gathered(routes, acts, grads, weights, cluster)


def solution(mesh):
    return jax.shard_map(
        on_device,
        mesh=mesh,
        in_specs=(
            P(("groups", "expert"), None),
            P(("groups", "expert"), None),
            P(("groups", "expert"), None, None),
            P(("groups", "expert"), None, None),
            P("groups"),
        ),
        out_specs=P("groups", "expert", None),
        check_vma=False,
    )
```
